32 devices in a mesh: dp: 8 (over z, y), nbr: 4 (over x, core).
Axes of the slice: x: 2, y: 2, z: 4, core: 2. Of those that a mesh axis runs over, the one named last changes fastest.
Arguments:
- queries: bfloat16 [6144, 4096], P(('dp', 'nbr')), may hold values from -256 to 256
- cotangent: bfloat16 [6144, 4096], P(('dp', 'nbr')), may hold values from -1 to 1
- pool: bfloat16 [64, 128, 896], P('dp', 'nbr'), may hold values from -60 to 60
- enc_gain: float32 [896], replicated, may hold values from 0.25 to 1.75
- enc_weight: bfloat16 [896, 896], replicated, may hold values from -0.1875 to 0.1875
- k_weight: bfloat16 [896, 4096], P(None, 'nbr'), may hold values from -0.1875 to 0.1875
- v_weight: bfloat16 [896, 4096], P(None, 'nbr'), may hold values from -0.1875 to 0.1875
- nbr_owner: int32 [96, 1], replicated, may hold values from 0 to 7; in each aligned block of 12 rows (0 to 11, 12 to 23, ...) at most 2 rows name the same one
- nbr_slot: int32 [96, 1], replicated, may hold values from 0 to 7
Outputs:
- attended: bfloat16 [6144, 4096], P(('dp', 'nbr'))
- grad_k: float32 [896, 4096], P('dp', 'nbr')
- grad_v: float32 [896, 4096], P('dp', 'nbr')
The draws below stay inside these ranges and needn't reach their ends.
Inputs may be any that keep to these rules, and one draw needn't show every extreme that they name: `nbr_owner`: within the 12 groups of one sequence at most 2 name the same index of dp, and this bound is reached.
All inputs are finite; a program needn't handle non-finite values.
Results may differ from the reference program's by a relative error of at most 0.035.
The reference program's roundings to bfloat16 on the way (of `normed`, `encoded`, `neighbours` and `weights`) count: a program that leaves them out, or rounds other values in their place, can miss the bound.
Values may be sent and summed in bfloat16 or wider, within the bound.
A program may use at most 128 MiB of HBM per device.

```python
import math
import jax
import jax.numpy as jnp
import numpy as np
from jax import lax

D = 4096
HEADS = 32
HEAD = 128
E = 896
GROUP = 64
RL = 128
KN = 1
CAP = 2
NB = 8
LEN = 768
CH_ROW = 12
TOKENS = 6144
GROUPS = 96
POOL = 64
N_DP = 8


def draw_queries(key, part):
    base_key = jax.random.fold_in(key, 0)
    base = jnp.clip(jax.random.normal(base_key, (TOKENS, D), jnp.float32), -6.0, 6.0)
    return base.astype(jnp.bfloat16)


def draw_pool(key, part):
    base_key, row_key, col_key = jax.random.split(key, 3)
    base = jnp.clip(jax.random.normal(base_key, (POOL, RL, E), jnp.float32), -6.0, 6.0)
    lower, upper = (0.1, 1.0)
    row_scale = jnp.exp(jax.random.uniform(row_key, (POOL, RL, 1), jnp.float32, math.log(lower), math.log(upper)))
    col_scale = jnp.exp(jax.random.uniform(col_key, (1, 1, E), jnp.float32, math.log(lower), math.log(upper)))
    return (base * row_scale * col_scale).astype(jnp.bfloat16)


def with_ends(drawn, own_key, smallest, largest):
    longest = drawn.shape.index(max(drawn.shape))
    spots = []
    for shift in (0, 1):
        where = [jax.random.randint(jax.random.fold_in(own_key, axis), (), 0, length) for axis, length in enumerate(drawn.shape)]
        where[longest] = (where[longest] + shift) % drawn.shape[longest]
        spots.append(tuple(where))
    return drawn.at[spots[0]].set(smallest).at[spots[1]].set(largest)


def shard_levels(own_key, dims, shards, low, top_value):
    loudness = 1.0
    for dim, parts in shards:
        draws = jax.random.uniform(jax.random.fold_in(jax.random.fold_in(own_key, 6), dim), (parts,), jnp.float32, low / len(shards), top_value / len(shards))
        loudness = loudness * jnp.repeat(jnp.exp(draws), dims[dim] // parts).reshape((-1,) + (1,) * (len(dims) - 1 - dim))
    return loudness


def shared_out(key, own, number, rows, count, top, limit, slope):
    order = jax.random.permutation(key, count)
    crowded, ordinary = portions_of(count, rows * top, limit, slope, True), portions_of(count, rows * top, limit, slope, False)
    places = jnp.arange(count)

    def named(tallies, turn):
        used = int((tallies > 0).sum())
        fixed = max(1, used // 4)
        moved = fixed + (places - fixed + turn * (used - fixed)) % max(1, count - fixed)
        return jnp.zeros((count,), jnp.int32).at[order[jnp.where(places < fixed, places, moved)]].set(jnp.asarray(tallies, jnp.int32))

    tallies = jnp.where(number % 4 == 0, named(crowded, number // 4), named(ordinary, number - number // 4 - 1))
    mixed = jax.random.permutation(jax.random.fold_in(own, 3), count)
    donor, receiver = mixed[0:count // 2 * 2:2], mixed[1:count // 2 * 2:2]
    margin = jnp.minimum(tallies[donor] - 1, limit - tallies[receiver]) // 2
    margin = jnp.where((donor == order[0]) | (receiver == order[0]) | (tallies[receiver] == 0), 0, jnp.maximum(margin, 0))
    moved = jax.random.randint(jax.random.fold_in(own, 4), (count // 2,), 0, 1 << 20) % (margin + 1)
    tallies = tallies.at[donor].add(-moved).at[receiver].add(moved)
    items = jnp.searchsorted(jnp.cumsum(tallies), jnp.arange(rows * top), side="right").astype(jnp.int32)
    grid = items.reshape(top, rows).T
    grid = grid[jax.random.permutation(jax.random.fold_in(own, 1), rows)]
    turn = jax.random.randint(jax.random.fold_in(own, 2), (rows, 1), 0, top)
    return jnp.take_along_axis(grid, (jnp.arange(top)[None, :] + turn) % top, axis=1)


def portions_of(count, total, limit, slope, full):
    portions = [(1 << 20) // math.isqrt(grade ** slope) + 1 for grade in range(1, count + 1)]
    largest = limit if full else min(limit, max(-(-total // count), total * portions[0] // sum(portions)))
    least = 1 if total - largest >= count - 1 else 0
    holding, surplus = [largest] + [least] * (count - 1), total - largest - least * (count - 1)
    while surplus > 0:
        movable = [i for i in range(1, count) if holding[i] < largest] or [i for i in range(1, count) if holding[i] < limit]
        whole, budget = sum([portions[i] for i in movable]), surplus
        for i in movable:
            addition = min(limit - holding[i], max(1, budget * portions[i] // whole), surplus)
            holding[i] = holding[i] + addition
            surplus = surplus - addition
    return np.array(holding)


def normal_values(key, extent, scale, limit, shards=(), kind=jnp.bfloat16):
    drawn = jax.random.normal(key, extent, jnp.float32) * scale
    if len(shards) > 0:
        drawn = shard_levels(key, extent, shards, -0.22, 0.18) * drawn
    return jnp.clip(drawn, min=-limit, max=limit).astype(kind)


def setup_inputs(seed: int = 0) -> dict:
    arg_keys = jax.random.split(jax.random.key(seed), 10)
    queries = draw_queries(jax.random.fold_in(arg_keys[9], 71), 0)
    cotangent = normal_values(arg_keys[1], (TOKENS, D), 0.0625, 1.0, ((0, 32),))
    pool = draw_pool(jax.random.fold_in(arg_keys[9], 71), 0)
    enc_gain = jnp.clip(1.0 + 0.15 * jax.random.normal(arg_keys[3], (E,), jnp.float32), 0.25, 1.75)
    enc_weight = normal_values(arg_keys[4], (E, E), E ** -0.5, 0.1875)
    k_weight = normal_values(arg_keys[5], (E, D), E ** -0.5, 0.1875, ((1, 4),))
    v_weight = normal_values(arg_keys[6], (E, D), E ** -0.5, 0.1875, ((1, 4),))
    nbr_owner_keys = jax.random.split(jax.random.fold_in(arg_keys[7], 1), GROUPS // CH_ROW)
    nbr_owner_turns = jax.random.permutation(jax.random.fold_in(arg_keys[7], 3), GROUPS // CH_ROW)
    nbr_owner = jax.vmap(lambda own, number: shared_out(jax.random.fold_in(arg_keys[7], 2), own, number, CH_ROW, N_DP, KN, CAP, 2))(nbr_owner_keys, nbr_owner_turns).reshape((GROUPS, KN))
    nbr_slot = with_ends(jax.random.randint(arg_keys[8], (GROUPS, KN), 0, NB), jax.random.fold_in(arg_keys[8], 1), 0, NB - 1).astype(jnp.int32)
    return {"queries": queries, "cotangent": cotangent, "pool": pool, "enc_gain": enc_gain, "enc_weight": enc_weight, "k_weight": k_weight, "v_weight": v_weight, "nbr_owner": nbr_owner, "nbr_slot": nbr_slot}


def encode(blocks, gain_vec, weight):
    widened = blocks.astype(jnp.float32)
    mean_sq = lax.optimization_barrier(jnp.mean(widened * widened, axis=-1, keepdims=True))
    normed = (widened * lax.rsqrt(mean_sq + 1e-06) * gain_vec).astype(jnp.bfloat16)
    feature_width = blocks.shape[-1]
    combined = jnp.dot(normed.reshape(-1, feature_width), weight, preferred_element_type=jnp.float32)
    return (widened + jax.nn.gelu(combined.reshape(widened.shape))).astype(jnp.bfloat16)

def attend(q_heads, key_rows, value_rows, group_len):
    offset_rows = group_len - 1
    seq_len, head_count, head_size = q_heads.shape
    blank_rows = jnp.zeros((offset_rows, head_count, head_size), q_heads.dtype)
    shifted = jnp.concatenate([q_heads[offset_rows:], blank_rows], axis=0)
    shifted = shifted.reshape(-1, group_len, head_count, head_size)
    scores = jnp.einsum('cqhd,ckhd->chqk', shifted.astype(jnp.float32), key_rows.astype(jnp.float32))
    scores = scores * head_size ** (-0.5)
    weights = jax.nn.softmax(scores, axis=-1).astype(jnp.bfloat16)
    combined = jnp.einsum('chqk,ckhd->cqhd', weights.astype(jnp.float32), value_rows.astype(jnp.float32))
    combined = combined.astype(jnp.bfloat16).reshape(seq_len, head_count, head_size)
    return jnp.concatenate([blank_rows, combined[:seq_len - offset_rows]], axis=0)

def reference(queries, cotangent, pool, enc_gain, enc_weight, k_weight, v_weight, nbr_owner, nbr_slot):
    encoded = encode(pool, enc_gain, enc_weight)
    block_ids = (nbr_owner * NB + nbr_slot)[:, 0].astype(jnp.int32)

    def sequence_step(totals, seq_index):
        first_row = seq_index * LEN
        q_rows = lax.dynamic_slice_in_dim(queries, first_row, LEN, 0)
        g_rows = lax.dynamic_slice_in_dim(cotangent, first_row, LEN, 0)
        chosen = lax.dynamic_slice_in_dim(block_ids, seq_index * CH_ROW, CH_ROW, 0)
        neighbours = jnp.take(encoded, chosen, axis=0)
        flat_enc = neighbours.reshape(CH_ROW * RL, E)
        key_rows = jnp.dot(flat_enc, k_weight, preferred_element_type=jnp.float32).astype(jnp.bfloat16)
        value_rows = jnp.dot(flat_enc, v_weight, preferred_element_type=jnp.float32).astype(jnp.bfloat16)
        q_heads = q_rows.reshape(LEN, HEADS, HEAD)

        def attend_here(keys_in, values_in):
            shaped_keys = keys_in.reshape(CH_ROW, RL, HEADS, HEAD)
            shaped_values = values_in.reshape(CH_ROW, RL, HEADS, HEAD)
            return attend(q_heads, shaped_keys, shaped_values, GROUP).reshape(LEN, D)
        attended, pullback = jax.vjp(attend_here, key_rows, value_rows)
        key_grads, value_grads = pullback(g_rows)
        grad_key = jnp.dot(flat_enc.T, key_grads, preferred_element_type=jnp.float32)
        grad_value = jnp.dot(flat_enc.T, value_grads, preferred_element_type=jnp.float32)
        return ((totals[0] + grad_key, totals[1] + grad_value), attended)
    blank_grad = jnp.zeros((E, D), jnp.float32)
    totals, attended_all = lax.scan(sequence_step, (blank_grad, blank_grad), jnp.arange(N_DP).astype(jnp.int32))
    return (attended_all.reshape(TOKENS, D), totals[0], totals[1])
```

```python
import functools

import jax
import jax.numpy as jnp
from jax import lax
from jax.experimental import pallas as pl
from jax.experimental.pallas import tpu as pltpu
from jax.sharding import PartitionSpec as P

HEAD = 128
GROUP = 64
CAP = 2
BF = jnp.bfloat16
F32 = jnp.float32


def encode(blocks, gain_vec, weight):
    widened = blocks.astype(F32)
    mean_sq = jnp.mean(widened * widened, axis=-1, keepdims=True)
    normed = (widened * lax.rsqrt(mean_sq + 1e-06) * gain_vec).astype(BF)
    combined = jnp.dot(normed, weight, preferred_element_type=F32)
    return (widened + jax.nn.gelu(combined)).astype(BF)


def pick_rows(chosen, rows, tokens):
    m, n = chosen.shape
    eye = jnp.eye(tokens, dtype=BF)
    full = chosen.astype(BF)[:, None, :, None] * eye[None, :, None, :]
    full = full.reshape(m * tokens, n * tokens)
    return jnp.dot(full, rows, preferred_element_type=F32).astype(BF)


def attention_body(q_ref, g_ref, k_ref, v_ref, o_ref, dk_ref, dv_ref):
    heads = q_ref.shape[1] // HEAD
    parts, _, tokens, _ = k_ref.shape
    keys = parts * tokens
    scale = HEAD ** (-0.5)
    over_last = (((1,), (1,)), ((), ()))
    over_first = (((0,), (0,)), ((), ()))
    for h in range(heads):
        cols = slice(h * HEAD, (h + 1) * HEAD)
        q = q_ref[:, cols]
        g = g_ref[:, cols]
        k = k_ref[:, 0, :, cols].reshape(keys, HEAD)
        v = v_ref[:, 0, :, cols].reshape(keys, HEAD)
        s = lax.dot_general(q, k, over_last, preferred_element_type=F32) * scale
        e = jnp.exp(s - jnp.max(s, axis=-1, keepdims=True))
        p = e / jnp.sum(e, axis=-1, keepdims=True)
        w = p.astype(BF)
        o_ref[:, cols] = jnp.dot(w, v, preferred_element_type=F32).astype(BF)
        dw = lax.dot_general(g, v, over_last, preferred_element_type=F32)
        dw = dw.astype(BF).astype(F32)
        ds = p * (dw - jnp.sum(dw * p, axis=-1, keepdims=True)) * scale
        dk = lax.dot_general(ds.astype(BF), q, over_first, preferred_element_type=F32)
        dv = lax.dot_general(w, g, over_first, preferred_element_type=F32)
        dk_ref[:, 0, :, cols] = dk.astype(BF).reshape(parts, tokens, HEAD)
        dv_ref[:, 0, :, cols] = dv.astype(BF).reshape(parts, tokens, HEAD)


def attention(q, g, k, v):
    length, width = q.shape
    parts, groups, tokens, _ = k.shape
    row = pl.BlockSpec((GROUP, width), lambda c: (c, 0))
    block = pl.BlockSpec((parts, 1, tokens, width), lambda c: (0, c, 0, 0))
    work = 10 * length * parts * tokens * width
    return pl.pallas_call(
        attention_body,
        grid=(groups,),
        in_specs=[row, row, block, block],
        out_specs=[row, block, block],
        out_shape=[
            jax.ShapeDtypeStruct(q.shape, BF),
            jax.ShapeDtypeStruct(k.shape, BF),
            jax.ShapeDtypeStruct(v.shape, BF),
        ],
        compiler_params=pltpu.CompilerParams(vmem_limit_bytes=32 * 2**20),
        cost_estimate=pl.CostEstimate(
            flops=work,
            bytes_accessed=6 * length * width + 8 * k.size,
            transcendentals=length * parts * tokens * width // HEAD,
        ),
    )(q, g, k, v)


def per_device(
    queries, cotangent, pool, enc_gain, enc_weight, k_weight, v_weight, nbr_owner, nbr_slot
):
    dp_count = lax.axis_size("dp")
    nbr_count = lax.axis_size("nbr")
    me = lax.axis_index("dp")
    held, tokens, enc_width = pool.shape
    per_row = nbr_owner.shape[0] // dp_count

    owners = nbr_owner[:, 0].reshape(dp_count, per_row)
    slots = nbr_slot[:, 0].reshape(dp_count, per_row)
    same = owners[:, :, None] == owners[:, None, :]
    earlier = jnp.tril(jnp.ones((per_row, per_row), jnp.bool_), -1)
    rank = jnp.sum((same & earlier[None]).astype(jnp.int32), axis=-1)

    ranks = jnp.arange(CAP, dtype=jnp.int32)
    blocks = jnp.arange(held, dtype=jnp.int32)
    mine = (owners == me)[:, None, :] & (rank[:, None, :] == ranks[None, :, None])
    send = jnp.any(
        mine[:, :, None, :] & (slots[:, None, None, :] == blocks[None, None, :, None]), axis=-1
    ).reshape(dp_count * CAP, held)
    enc = encode(pool.reshape(held * tokens, enc_width), enc_gain, enc_weight)
    outgoing = pick_rows(send, enc, tokens)
    arrived = lax.all_to_all(outgoing, "dp", split_axis=0, concat_axis=0, tiled=True)

    place = lax.dynamic_slice_in_dim(owners * CAP + rank, me, 1, 0)[0]
    take = place[:, None] == jnp.arange(dp_count * CAP, dtype=jnp.int32)[None, :]
    picked = pick_rows(take, arrived, tokens)
    flat_enc = lax.all_gather(picked, "nbr", axis=0, tiled=True)

    q_rows = lax.all_to_all(queries, "nbr", split_axis=1, concat_axis=0, tiled=True)
    g_rows = lax.all_to_all(cotangent, "nbr", split_axis=1, concat_axis=0, tiled=True)
    seq_len, width = q_rows.shape
    lead = GROUP - 1
    blank = jnp.zeros((lead, width), BF)
    q_rows = jnp.concatenate([q_rows[lead:], blank], axis=0)
    g_rows = jnp.concatenate([g_rows[lead:], blank], axis=0)

    shape4 = (nbr_count, per_row, tokens, width)
    keys = jnp.dot(flat_enc, k_weight, preferred_element_type=F32).astype(BF)
    values = jnp.dot(flat_enc, v_weight, preferred_element_type=F32).astype(BF)
    out, dk, dv = attention(q_rows, g_rows, keys.reshape(shape4), values.reshape(shape4))

    over_first = (((0,), (0,)), ((), ()))

    def weight_grad(grads):
        product = lax.dot_general(
            flat_enc, grads.reshape(-1, width), over_first, preferred_element_type=F32
        )
        return lax.psum_scatter(
            product.astype(BF), "dp", scatter_dimension=0, tiled=True
        ).astype(F32)

    grad_v = weight_grad(dv)
    grad_k = weight_grad(dk)
    out = jnp.concatenate([blank, out[: seq_len - lead]], axis=0)
    merged = lax.all_to_all(out, "nbr", split_axis=0, concat_axis=1, tiled=True)
    return (merged, grad_k, grad_v)


def solution(mesh):
    return jax.shard_map(
        per_device,
        mesh=mesh,
        in_specs=(
            P(("dp", "nbr"), None),
            P(("dp", "nbr"), None),
            P("dp", "nbr", None),
            P(),
            P(),
            P(None, "nbr"),
            P(None, "nbr"),
            P(),
            P(),
        ),
        out_specs=(P(("dp", "nbr"), None), P("dp", "nbr"), P("dp", "nbr")),
        check_vma=False,
    )
```

```python
import jax
import jax.numpy as jnp
from jax import lax
from jax.experimental import pallas as pl
from jax.experimental.pallas import tpu as pltpu
from jax.sharding import PartitionSpec as P

HEAD = 128
GROUP = 64
CAP = 2
BF = jnp.bfloat16
F32 = jnp.float32


def encode(blocks, gain_vec, weight):
    widened = blocks.astype(F32)
    mean_sq = jnp.mean(widened * widened, axis=-1, keepdims=True)
    normed = (widened * lax.rsqrt(mean_sq + 1e-06) * gain_vec).astype(BF)
    combined = jnp.dot(normed, weight, preferred_element_type=F32)
    return (widened + jax.nn.gelu(combined)).astype(BF)


def pick_rows(chosen, rows, tokens):
    m, n = chosen.shape
    eye = jnp.eye(tokens, dtype=BF)
    full = chosen.astype(BF)[:, None, :, None] * eye[None, :, None, :]
    full = full.reshape(m * tokens, n * tokens)
    return jnp.dot(full, rows, preferred_element_type=F32).astype(BF)


def attention_body(q_ref, g_ref, k_ref, v_ref, o_ref, dk_ref, dv_ref):
    heads = q_ref.shape[1] // HEAD
    parts, _, tokens, _ = k_ref.shape
    keys = parts * tokens
    scale = HEAD ** (-0.5)
    over_last = (((1,), (1,)), ((), ()))
    over_first = (((0,), (0,)), ((), ()))
    for first in range(0, heads, 4):
        held = []
        for h in range(first, min(first + 4, heads)):
            cols = slice(h * HEAD, (h + 1) * HEAD)
            k = k_ref[:, 0, :, cols].reshape(keys, HEAD)
            v = v_ref[:, 0, :, cols].reshape(keys, HEAD)
            s = lax.dot_general(q_ref[:, cols], k, over_last, preferred_element_type=F32)
            dw = lax.dot_general(g_ref[:, cols], v, over_last, preferred_element_type=F32)
            held.append((cols, v, s * scale, dw.astype(BF).astype(F32)))
        ready = []
        for cols, v, s, dw in held:
            e = jnp.exp(s - jnp.max(s, axis=-1, keepdims=True))
            p = e * (1.0 / jnp.sum(e, axis=-1, keepdims=True))
            ds = p * (dw - jnp.sum(dw * p, axis=-1, keepdims=True)) * scale
            ready.append((cols, v, p.astype(BF), ds.astype(BF)))
        for cols, v, w, ds in ready:
            q, g = q_ref[:, cols], g_ref[:, cols]
            o_ref[:, cols] = jnp.dot(w, v, preferred_element_type=F32).astype(BF)
            dk = lax.dot_general(ds, q, over_first, preferred_element_type=F32)
            dv = lax.dot_general(w, g, over_first, preferred_element_type=F32)
            dk_ref[:, 0, :, cols] = dk.astype(BF).reshape(parts, tokens, HEAD)
            dv_ref[:, 0, :, cols] = dv.astype(BF).reshape(parts, tokens, HEAD)


def attention(q, g, k, v):
    length, width = q.shape
    parts, groups, tokens, _ = k.shape
    row = pl.BlockSpec((GROUP, width), lambda c: (c, 0))
    block = pl.BlockSpec((parts, 1, tokens, width), lambda c: (0, c, 0, 0))
    work = 10 * length * parts * tokens * width
    return pl.pallas_call(
        attention_body,
        grid=(groups,),
        in_specs=[row, row, block, block],
        out_specs=[row, block, block],
        out_shape=[
            jax.ShapeDtypeStruct(q.shape, BF),
            jax.ShapeDtypeStruct(k.shape, BF),
            jax.ShapeDtypeStruct(v.shape, BF),
        ],
        compiler_params=pltpu.CompilerParams(vmem_limit_bytes=32 * 2**20),
        cost_estimate=pl.CostEstimate(
            flops=work,
            bytes_accessed=6 * length * width + 8 * k.size,
            transcendentals=length * parts * tokens * width // HEAD,
        ),
    )(q, g, k, v)


def exchange(x, axis, split, join):
    n = lax.axis_size(axis)
    me = lax.axis_index(axis)
    span = x.shape[split] // n
    step = x.shape[join]
    parts = []
    for d in range(n):
        piece = lax.dynamic_slice_in_dim(x, (me ^ d) * span, span, split)
        if d:
            piece = lax.ppermute(piece, axis, [(i, i ^ d) for i in range(n)])
        parts.append(piece)
    shape = list(parts[0].shape)
    shape[join] = n * step
    whole = jnp.zeros(shape, x.dtype)
    for d, piece in enumerate(parts):
        whole = lax.dynamic_update_slice_in_dim(whole, piece, (me ^ d) * step, join)
    return whole


def halving(total, axis, turn):
    n = lax.axis_size(axis)
    me = lax.axis_index(axis)
    count = n.bit_length() - 1
    bits = [(i + turn) % count for i in range(count)]
    rows, width = total.shape
    current = total.reshape((2,) * count + (rows // n, width))
    left = list(range(count - 1, -1, -1))
    for bit in bits:
        place = left.index(bit)
        left.pop(place)
        mine = (me >> bit) & 1
        away = lax.dynamic_index_in_dim(current, 1 - mine, place, keepdims=False)
        keep = lax.dynamic_index_in_dim(current, mine, place, keepdims=False)
        pairs = [(i, i ^ (1 << bit)) for i in range(n)]
        current = keep + lax.ppermute(away.astype(BF), axis, pairs).astype(F32)
    return current


def per_device(
    queries, cotangent, pool, enc_gain, enc_weight, k_weight, v_weight, nbr_owner, nbr_slot
):
    dp_count = lax.axis_size("dp")
    nbr_count = lax.axis_size("nbr")
    me = lax.axis_index("dp")
    held, tokens, enc_width = pool.shape
    per_row = nbr_owner.shape[0] // dp_count

    owners = nbr_owner[:, 0].reshape(dp_count, per_row)
    slots = nbr_slot[:, 0].reshape(dp_count, per_row)
    same = owners[:, :, None] == owners[:, None, :]
    earlier = jnp.tril(jnp.ones((per_row, per_row), jnp.bool_), -1)
    rank = jnp.sum((same & earlier[None]).astype(jnp.int32), axis=-1)

    ranks = jnp.arange(CAP, dtype=jnp.int32)
    blocks = jnp.arange(held, dtype=jnp.int32)
    mine = (owners == me)[:, None, :] & (rank[:, None, :] == ranks[None, :, None])
    send = jnp.any(
        mine[:, :, None, :] & (slots[:, None, None, :] == blocks[None, None, :, None]), axis=-1
    ).reshape(dp_count * CAP, held)
    enc = encode(pool.reshape(held * tokens, enc_width), enc_gain, enc_weight)
    outgoing = pick_rows(send, enc, tokens)
    arrived = lax.all_to_all(outgoing, "dp", split_axis=0, concat_axis=0, tiled=True)

    place = lax.dynamic_slice_in_dim(owners * CAP + rank, me, 1, 0)[0]
    take = place[:, None] == jnp.arange(dp_count * CAP, dtype=jnp.int32)[None, :]
    picked = pick_rows(take, arrived, tokens)
    flat_enc = lax.all_gather(picked, "nbr", axis=0, tiled=True)

    q_rows = exchange(queries, "nbr", 1, 0)
    g_rows = exchange(cotangent, "nbr", 1, 0)
    seq_len, width = q_rows.shape
    lead = GROUP - 1
    blank = jnp.zeros((lead, width), BF)
    q_rows = jnp.concatenate([q_rows[lead:], blank], axis=0)
    g_rows = jnp.concatenate([g_rows[lead:], blank], axis=0)

    shape4 = (nbr_count, per_row, tokens, width)
    keys = jnp.dot(flat_enc, k_weight, preferred_element_type=F32).astype(BF)
    values = jnp.dot(flat_enc, v_weight, preferred_element_type=F32).astype(BF)
    out, dk, dv = attention(q_rows, g_rows, keys.reshape(shape4), values.reshape(shape4))

    over_first = (((0,), (0,)), ((), ()))

    def weight_grad(grads, turn):
        product = lax.dot_general(
            flat_enc, grads.reshape(-1, width), over_first, preferred_element_type=F32
        )
        return halving(product, "dp", turn)

    grad_v = weight_grad(dv, 0)
    grad_k = weight_grad(dk, 1)
    out = jnp.concatenate([blank, out[: seq_len - lead]], axis=0)
    merged = exchange(out, "nbr", 0, 1)
    return (merged, grad_k, grad_v)


def solution(mesh):
    return jax.shard_map(
        per_device,
        mesh=mesh,
        in_specs=(
            P(("dp", "nbr"), None),
            P(("dp", "nbr"), None),
            P("dp", "nbr", None),
            P(),
            P(),
            P(None, "nbr"),
            P(None, "nbr"),
            P(),
            P(),
        ),
        out_specs=(P(("dp", "nbr"), None), P("dp", "nbr"), P("dp", "nbr")),
        check_vma=False,
    )
```

```python
import jax
import jax.numpy as jnp
from jax import lax
from jax.experimental import pallas as pl
from jax.experimental.pallas import tpu as pltpu
from jax.sharding import PartitionSpec as P

HEAD = 128
GROUP = 64
CAP = 2
BF = jnp.bfloat16
F32 = jnp.float32


def encode(blocks, gain_vec, weight):
    widened = blocks.astype(F32)
    mean_sq = jnp.mean(widened * widened, axis=-1, keepdims=True)
    normed = (widened * lax.rsqrt(mean_sq + 1e-06) * gain_vec).astype(BF)
    combined = jnp.dot(normed, weight, preferred_element_type=F32)
    return (widened + jax.nn.gelu(combined)).astype(BF)


def pick_rows(chosen, rows, tokens):
    m, n = chosen.shape
    eye = jnp.eye(tokens, dtype=BF)
    full = chosen.astype(BF)[:, None, :, None] * eye[None, :, None, :]
    full = full.reshape(m * tokens, n * tokens)
    return jnp.dot(full, rows, preferred_element_type=F32).astype(BF)


def attention_body(q_ref, g_ref, k_ref, v_ref, o_ref, dk_ref, dv_ref):
    heads = q_ref.shape[1] // HEAD
    parts, _, tokens, _ = k_ref.shape
    keys = parts * tokens
    scale = HEAD ** (-0.5)
    over_last = (((1,), (1,)), ((), ()))
    over_first = (((0,), (0,)), ((), ()))
    for first in range(0, heads, 4):
        held = []
        for h in range(first, min(first + 4, heads)):
            cols = slice(h * HEAD, (h + 1) * HEAD)
            k = k_ref[:, 0, :, cols].reshape(keys, HEAD)
            v = v_ref[:, 0, :, cols].reshape(keys, HEAD)
            s = lax.dot_general(q_ref[:, cols], k, over_last, preferred_element_type=F32)
            dw = lax.dot_general(g_ref[:, cols], v, over_last, preferred_element_type=F32)
            held.append((cols, v, s * scale, dw.astype(BF).astype(F32)))
        ready = []
        for cols, v, s, dw in held:
            e = jnp.exp(s - jnp.max(s, axis=-1, keepdims=True))
            p = e * (1.0 / jnp.sum(e, axis=-1, keepdims=True))
            ds = p * (dw - jnp.sum(dw * p, axis=-1, keepdims=True)) * scale
            ready.append((cols, v, p.astype(BF), ds.astype(BF)))
        for cols, v, w, ds in ready:
            q, g = q_ref[:, cols], g_ref[:, cols]
            o_ref[:, cols] = jnp.dot(w, v, preferred_element_type=F32).astype(BF)
            dk = lax.dot_general(ds, q, over_first, preferred_element_type=F32)
            dv = lax.dot_general(w, g, over_first, preferred_element_type=F32)
            dk_ref[:, 0, :, cols] = dk.astype(BF).reshape(parts, tokens, HEAD)
            dv_ref[:, 0, :, cols] = dv.astype(BF).reshape(parts, tokens, HEAD)


def attention(q, g, k, v):
    length, width = q.shape
    parts, groups, tokens, _ = k.shape
    row = pl.BlockSpec((GROUP, width), lambda c: (c, 0))
    block = pl.BlockSpec((parts, 1, tokens, width), lambda c: (0, c, 0, 0))
    work = 10 * length * parts * tokens * width
    return pl.pallas_call(
        attention_body,
        grid=(groups,),
        in_specs=[row, row, block, block],
        out_specs=[row, block, block],
        out_shape=[
            jax.ShapeDtypeStruct(q.shape, BF),
            jax.ShapeDtypeStruct(k.shape, BF),
            jax.ShapeDtypeStruct(v.shape, BF),
        ],
        compiler_params=pltpu.CompilerParams(vmem_limit_bytes=32 * 2**20),
        cost_estimate=pl.CostEstimate(
            flops=work,
            bytes_accessed=6 * length * width + 8 * k.size,
            transcendentals=length * parts * tokens * width // HEAD,
        ),
    )(q, g, k, v)


def exchange(x, axis, split, join):
    n = lax.axis_size(axis)
    me = lax.axis_index(axis)
    span = x.shape[split] // n
    step = x.shape[join]
    parts = []
    for d in range(n):
        piece = lax.dynamic_slice_in_dim(x, (me ^ d) * span, span, split)
        if d:
            piece = lax.ppermute(piece, axis, [(i, i ^ d) for i in range(n)])
        parts.append(piece)
    shape = list(parts[0].shape)
    shape[join] = n * step
    whole = jnp.zeros(shape, x.dtype)
    for d, piece in enumerate(parts):
        whole = lax.dynamic_update_slice_in_dim(whole, piece, (me ^ d) * step, join)
    return whole


def halving(total, axis, turn):
    n = lax.axis_size(axis)
    me = lax.axis_index(axis)
    count = n.bit_length() - 1
    bits = [(i + turn) % count for i in range(count)]
    rows, width = total.shape
    current = total.reshape((2,) * count + (rows // n, width))
    left = list(range(count - 1, -1, -1))
    for bit in bits:
        place = left.index(bit)
        left.pop(place)
        mine = (me >> bit) & 1
        away = lax.dynamic_index_in_dim(current, 1 - mine, place, keepdims=False)
        keep = lax.dynamic_index_in_dim(current, mine, place, keepdims=False)
        pairs = [(i, i ^ (1 << bit)) for i in range(n)]
        current = keep + lax.ppermute(away.astype(BF), axis, pairs).astype(F32)
    return current


def per_device(
    queries, cotangent, pool, enc_gain, enc_weight, k_weight, v_weight, nbr_owner, nbr_slot
):
    dp_count = lax.axis_size("dp")
    nbr_count = lax.axis_size("nbr")
    me = lax.axis_index("dp")
    held, tokens, enc_width = pool.shape
    per_row = nbr_owner.shape[0] // dp_count

    owners = nbr_owner[:, 0].reshape(dp_count, per_row)
    slots = nbr_slot[:, 0].reshape(dp_count, per_row)
    same = owners[:, :, None] == owners[:, None, :]
    earlier = jnp.tril(jnp.ones((per_row, per_row), jnp.bool_), -1)
    rank = jnp.sum((same & earlier[None]).astype(jnp.int32), axis=-1)

    ranks = jnp.arange(CAP, dtype=jnp.int32)
    blocks = jnp.arange(held, dtype=jnp.int32)
    mine = (owners == me)[:, None, :] & (rank[:, None, :] == ranks[None, :, None])
    send = jnp.any(
        mine[:, :, None, :] & (slots[:, None, None, :] == blocks[None, None, :, None]), axis=-1
    ).reshape(dp_count * CAP, held)
    enc = encode(pool.reshape(held * tokens, enc_width), enc_gain, enc_weight)
    outgoing = pick_rows(send, enc, tokens)
    arrived = lax.all_to_all(outgoing, "dp", split_axis=0, concat_axis=0, tiled=True)

    q_rows = exchange(queries, "nbr", 1, 0)
    arrived, q_rows = lax.optimization_barrier((arrived, q_rows))

    place = lax.dynamic_slice_in_dim(owners * CAP + rank, me, 1, 0)[0]
    take = place[:, None] == jnp.arange(dp_count * CAP, dtype=jnp.int32)[None, :]
    picked = pick_rows(take, arrived, tokens)
    flat_enc = lax.all_gather(picked, "nbr", axis=0, tiled=True)

    g_rows = exchange(cotangent, "nbr", 1, 0)
    seq_len, width = q_rows.shape
    lead = GROUP - 1
    blank = jnp.zeros((lead, width), BF)
    q_rows = jnp.concatenate([q_rows[lead:], blank], axis=0)
    g_rows = jnp.concatenate([g_rows[lead:], blank], axis=0)

    shape4 = (nbr_count, per_row, tokens, width)
    keys = jnp.dot(flat_enc, k_weight, preferred_element_type=F32).astype(BF)
    values = jnp.dot(flat_enc, v_weight, preferred_element_type=F32).astype(BF)
    out, dk, dv = attention(q_rows, g_rows, keys.reshape(shape4), values.reshape(shape4))

    over_first = (((0,), (0,)), ((), ()))

    def weight_grad(grads):
        return lax.dot_general(
            flat_enc, grads.reshape(-1, width), over_first, preferred_element_type=F32
        )

    grad_v = halving(weight_grad(dv), "dp", 0)
    product_k = weight_grad(dk)
    cut = width // HEAD * 3 // 8 * HEAD
    grad_k = jnp.concatenate(
        [halving(product_k[:, :cut], "dp", 0), halving(product_k[:, cut:], "dp", 1)], axis=1
    )
    out = jnp.concatenate([blank, out[: seq_len - lead]], axis=0)
    merged = exchange(out, "nbr", 0, 1)
    return (merged, grad_k, grad_v)


def solution(mesh):
    return jax.shard_map(
        per_device,
        mesh=mesh,
        in_specs=(
            P(("dp", "nbr"), None),
            P(("dp", "nbr"), None),
            P("dp", "nbr", None),
            P(),
            P(),
            P(None, "nbr"),
            P(None, "nbr"),
            P(),
            P(),
        ),
        out_specs=(P(("dp", "nbr"), None), P("dp", "nbr"), P("dp", "nbr")),
        check_vma=False,
    )
```

```python
import jax
import jax.numpy as jnp
from jax import lax
from jax.experimental import pallas as pl
from jax.experimental.pallas import tpu as pltpu
from jax.sharding import PartitionSpec as P

HEAD = 128
GROUP = 64
CAP = 2
BF = jnp.bfloat16
F32 = jnp.float32


def encode(blocks, gain_vec, weight):
    widened = blocks.astype(F32)
    mean_sq = jnp.mean(widened * widened, axis=-1, keepdims=True)
    normed = (widened * lax.rsqrt(mean_sq + 1e-06) * gain_vec).astype(BF)
    combined = jnp.dot(normed, weight, preferred_element_type=F32)
    return (widened + jax.nn.gelu(combined)).astype(BF)


def pick_rows(chosen, rows, tokens):
    m, n = chosen.shape
    eye = jnp.eye(tokens, dtype=BF)
    full = chosen.astype(BF)[:, None, :, None] * eye[None, :, None, :]
    full = full.reshape(m * tokens, n * tokens)
    return jnp.dot(full, rows, preferred_element_type=F32).astype(BF)


def attention_body(q_ref, g_ref, k_ref, v_ref, o_ref, dk_ref, dv_ref):
    heads = q_ref.shape[1] // HEAD
    parts, _, tokens, _ = k_ref.shape
    keys = parts * tokens
    scale = HEAD ** (-0.5)
    over_last = (((1,), (1,)), ((), ()))
    over_first = (((0,), (0,)), ((), ()))
    for first in range(0, heads, 4):
        held = []
        for h in range(first, min(first + 4, heads)):
            cols = slice(h * HEAD, (h + 1) * HEAD)
            k = k_ref[:, 0, :, cols].reshape(keys, HEAD)
            v = v_ref[:, 0, :, cols].reshape(keys, HEAD)
            s = lax.dot_general(q_ref[:, cols], k, over_last, preferred_element_type=F32)
            dw = lax.dot_general(g_ref[:, cols], v, over_last, preferred_element_type=F32)
            held.append((cols, v, s * scale, dw.astype(BF).astype(F32)))
        ready = []
        for cols, v, s, dw in held:
            e = jnp.exp(s - jnp.max(s, axis=-1, keepdims=True))
            p = e * (1.0 / jnp.sum(e, axis=-1, keepdims=True))
            ds = p * (dw - jnp.sum(dw * p, axis=-1, keepdims=True)) * scale
            ready.append((cols, v, p.astype(BF), ds.astype(BF)))
        for cols, v, w, ds in ready:
            q, g = q_ref[:, cols], g_ref[:, cols]
            o_ref[:, cols] = jnp.dot(w, v, preferred_element_type=F32).astype(BF)
            dk = lax.dot_general(ds, q, over_first, preferred_element_type=F32)
            dv = lax.dot_general(w, g, over_first, preferred_element_type=F32)
            dk_ref[:, 0, :, cols] = dk.astype(BF).reshape(parts, tokens, HEAD)
            dv_ref[:, 0, :, cols] = dv.astype(BF).reshape(parts, tokens, HEAD)


def attention(q, g, k, v):
    length, width = q.shape
    parts, groups, tokens, _ = k.shape
    row = pl.BlockSpec((GROUP, width), lambda c: (c, 0))
    block = pl.BlockSpec((parts, 1, tokens, width), lambda c: (0, c, 0, 0))
    work = 10 * length * parts * tokens * width
    return pl.pallas_call(
        attention_body,
        grid=(groups,),
        in_specs=[row, row, block, block],
        out_specs=[row, block, block],
        out_shape=[
            jax.ShapeDtypeStruct(q.shape, BF),
            jax.ShapeDtypeStruct(k.shape, BF),
            jax.ShapeDtypeStruct(v.shape, BF),
        ],
        compiler_params=pltpu.CompilerParams(vmem_limit_bytes=32 * 2**20),
        cost_estimate=pl.CostEstimate(
            flops=work,
            bytes_accessed=6 * length * width + 8 * k.size,
            transcendentals=length * parts * tokens * width // HEAD,
        ),
    )(q, g, k, v)


def exchange(x, axis, split, join):
    n = lax.axis_size(axis)
    me = lax.axis_index(axis)
    span = x.shape[split] // n
    step = x.shape[join]
    parts = []
    for d in range(n):
        piece = lax.dynamic_slice_in_dim(x, (me ^ d) * span, span, split)
        if d:
            piece = lax.ppermute(piece, axis, [(i, i ^ d) for i in range(n)])
        parts.append(piece)
    shape = list(parts[0].shape)
    shape[join] = n * step
    whole = jnp.zeros(shape, x.dtype)
    for d, piece in enumerate(parts):
        whole = lax.dynamic_update_slice_in_dim(whole, piece, (me ^ d) * step, join)
    return whole


def halving(total, axis, turn):
    n = lax.axis_size(axis)
    me = lax.axis_index(axis)
    count = n.bit_length() - 1
    bits = [(i + turn) % count for i in range(count)]
    rows, width = total.shape
    current = total.reshape((2,) * count + (rows // n, width))
    left = list(range(count - 1, -1, -1))
    for bit in bits:
        place = left.index(bit)
        left.pop(place)
        mine = (me >> bit) & 1
        away = lax.dynamic_index_in_dim(current, 1 - mine, place, keepdims=False)
        keep = lax.dynamic_index_in_dim(current, mine, place, keepdims=False)
        pairs = [(i, i ^ (1 << bit)) for i in range(n)]
        current = keep + lax.ppermute(away.astype(BF), axis, pairs).astype(F32)
    return current


def per_device(
    queries, cotangent, pool, enc_gain, enc_weight, k_weight, v_weight, nbr_owner, nbr_slot
):
    dp_count = lax.axis_size("dp")
    nbr_count = lax.axis_size("nbr")
    me = lax.axis_index("dp")
    held, tokens, enc_width = pool.shape
    per_row = nbr_owner.shape[0] // dp_count

    owners = nbr_owner[:, 0].reshape(dp_count, per_row)
    slots = nbr_slot[:, 0].reshape(dp_count, per_row)
    same = owners[:, :, None] == owners[:, None, :]
    earlier = jnp.tril(jnp.ones((per_row, per_row), jnp.bool_), -1)
    rank = jnp.sum((same & earlier[None]).astype(jnp.int32), axis=-1)

    ranks = jnp.arange(CAP, dtype=jnp.int32)
    blocks = jnp.arange(held, dtype=jnp.int32)
    mine = (owners == me)[:, None, :] & (rank[:, None, :] == ranks[None, :, None])
    send = jnp.any(
        mine[:, :, None, :] & (slots[:, None, None, :] == blocks[None, None, :, None]), axis=-1
    ).reshape(dp_count * CAP, held)
    enc = encode(pool.reshape(held * tokens, enc_width), enc_gain, enc_weight)
    outgoing = pick_rows(send, enc, tokens)
    arrived = lax.all_to_all(outgoing, "dp", split_axis=0, concat_axis=0, tiled=True)

    q_rows = exchange(queries, "nbr", 1, 0)
    g_rows = exchange(cotangent, "nbr", 1, 0)
    arrived, q_rows, g_rows = lax.optimization_barrier((arrived, q_rows, g_rows))

    place = lax.dynamic_slice_in_dim(owners * CAP + rank, me, 1, 0)[0]
    take = place[:, None] == jnp.arange(dp_count * CAP, dtype=jnp.int32)[None, :]
    picked = pick_rows(take, arrived, tokens)
    flat_enc = lax.all_gather(picked, "nbr", axis=0, tiled=True)

    seq_len, width = q_rows.shape
    lead = GROUP - 1
    blank = jnp.zeros((lead, width), BF)
    q_rows = jnp.concatenate([q_rows[lead:], blank], axis=0)
    g_rows = jnp.concatenate([g_rows[lead:], blank], axis=0)

    shape4 = (nbr_count, per_row, tokens, width)
    keys = jnp.dot(flat_enc, k_weight, preferred_element_type=F32).astype(BF)
    values = jnp.dot(flat_enc, v_weight, preferred_element_type=F32).astype(BF)
    out, dk, dv = attention(q_rows, g_rows, keys.reshape(shape4), values.reshape(shape4))

    over_first = (((0,), (0,)), ((), ()))

    def weight_grad(grads):
        return lax.dot_general(
            flat_enc, grads.reshape(-1, width), over_first, preferred_element_type=F32
        )

    grad_v = halving(weight_grad(dv), "dp", 0)
    product_k = weight_grad(dk)
    cut = width // HEAD * 3 // 8 * HEAD
    grad_k = jnp.concatenate(
        [halving(product_k[:, :cut], "dp", 0), halving(product_k[:, cut:], "dp", 1)], axis=1
    )
    out = jnp.concatenate([blank, out[: seq_len - lead]], axis=0)
    merged = exchange(out, "nbr", 0, 1)
    return (merged, grad_k, grad_v)


def solution(mesh):
    return jax.shard_map(
        per_device,
        mesh=mesh,
        in_specs=(
            P(("dp", "nbr"), None),
            P(("dp", "nbr"), None),
            P("dp", "nbr", None),
            P(),
            P(),
            P(None, "nbr"),
            P(None, "nbr"),
            P(),
            P(),
        ),
        out_specs=(P(("dp", "nbr"), None), P("dp", "nbr"), P("dp", "nbr")),
        check_vma=False,
    )
```

```python
import jax
import jax.numpy as jnp
from jax import lax
from jax.experimental import pallas as pl
from jax.experimental.pallas import tpu as pltpu
from jax.sharding import PartitionSpec as P

HEAD = 128
GROUP = 64
CAP = 2
BF = jnp.bfloat16
F32 = jnp.float32


def encode(blocks, gain_vec, weight):
    widened = blocks.astype(F32)
    mean_sq = jnp.mean(widened * widened, axis=-1, keepdims=True)
    normed = (widened * lax.rsqrt(mean_sq + 1e-06) * gain_vec).astype(BF)
    combined = jnp.dot(normed, weight, preferred_element_type=F32)
    return (widened + jax.nn.gelu(combined)).astype(BF)


def pick_rows(chosen, rows, tokens):
    m, n = chosen.shape
    eye = jnp.eye(tokens, dtype=BF)
    full = chosen.astype(BF)[:, None, :, None] * eye[None, :, None, :]
    full = full.reshape(m * tokens, n * tokens)
    return jnp.dot(full, rows, preferred_element_type=F32).astype(BF)


def attention_body(q_ref, g_ref, k_ref, v_ref, o_ref, dk_ref, dv_ref):
    heads = q_ref.shape[1] // HEAD
    parts, _, tokens, _ = k_ref.shape
    keys = parts * tokens
    scale = HEAD ** (-0.5)
    over_last = (((1,), (1,)), ((), ()))
    over_first = (((0,), (0,)), ((), ()))
    for first in range(0, heads, 4):
        held = []
        for h in range(first, min(first + 4, heads)):
            cols = slice(h * HEAD, (h + 1) * HEAD)
            k = k_ref[:, 0, :, cols].reshape(keys, HEAD)
            v = v_ref[:, 0, :, cols].reshape(keys, HEAD)
            s = lax.dot_general(q_ref[:, cols], k, over_last, preferred_element_type=F32)
            dw = lax.dot_general(g_ref[:, cols], v, over_last, preferred_element_type=F32)
            held.append((cols, v, s * scale, dw.astype(BF).astype(F32)))
        ready = []
        for cols, v, s, dw in held:
            e = jnp.exp(s - jnp.max(s, axis=-1, keepdims=True))
            p = e * (1.0 / jnp.sum(e, axis=-1, keepdims=True))
            ds = p * (dw - jnp.sum(dw * p, axis=-1, keepdims=True)) * scale
            ready.append((cols, v, p.astype(BF), ds.astype(BF)))
        for cols, v, w, ds in ready:
            q, g = q_ref[:, cols], g_ref[:, cols]
            o_ref[:, cols] = jnp.dot(w, v, preferred_element_type=F32).astype(BF)
            dk = lax.dot_general(ds, q, over_first, preferred_element_type=F32)
            dv = lax.dot_general(w, g, over_first, preferred_element_type=F32)
            dk_ref[:, 0, :, cols] = dk.astype(BF).reshape(parts, tokens, HEAD)
            dv_ref[:, 0, :, cols] = dv.astype(BF).reshape(parts, tokens, HEAD)


def attention(q, g, k, v):
    length, width = q.shape
    parts, groups, tokens, _ = k.shape
    row = pl.BlockSpec((GROUP, width), lambda c: (c, 0))
    block = pl.BlockSpec((parts, 1, tokens, width), lambda c: (0, c, 0, 0))
    work = 10 * length * parts * tokens * width
    return pl.pallas_call(
        attention_body,
        grid=(groups,),
        in_specs=[row, row, block, block],
        out_specs=[row, block, block],
        out_shape=[
            jax.ShapeDtypeStruct(q.shape, BF),
            jax.ShapeDtypeStruct(k.shape, BF),
            jax.ShapeDtypeStruct(v.shape, BF),
        ],
        compiler_params=pltpu.CompilerParams(vmem_limit_bytes=32 * 2**20),
        cost_estimate=pl.CostEstimate(
            flops=work,
            bytes_accessed=6 * length * width + 8 * k.size,
            transcendentals=length * parts * tokens * width // HEAD,
        ),
    )(q, g, k, v)


def exchange(x, axis, split, join):
    n = lax.axis_size(axis)
    me = lax.axis_index(axis)
    span = x.shape[split] // n
    step = x.shape[join]
    parts = []
    for d in range(n):
        piece = lax.dynamic_slice_in_dim(x, (me ^ d) * span, span, split)
        if d:
            piece = lax.ppermute(piece, axis, [(i, i ^ d) for i in range(n)])
        parts.append(piece)
    shape = list(parts[0].shape)
    shape[join] = n * step
    whole = jnp.zeros(shape, x.dtype)
    for d, piece in enumerate(parts):
        whole = lax.dynamic_update_slice_in_dim(whole, piece, (me ^ d) * step, join)
    return whole


def halving(total, axis, turn):
    n = lax.axis_size(axis)
    me = lax.axis_index(axis)
    count = n.bit_length() - 1
    bits = [(i + turn) % count for i in range(count)]
    rows, width = total.shape
    current = total.reshape((2,) * count + (rows // n, width))
    left = list(range(count - 1, -1, -1))
    for bit in bits:
        place = left.index(bit)
        left.pop(place)
        mine = (me >> bit) & 1
        away = lax.dynamic_index_in_dim(current, 1 - mine, place, keepdims=False)
        keep = lax.dynamic_index_in_dim(current, mine, place, keepdims=False)
        pairs = [(i, i ^ (1 << bit)) for i in range(n)]
        current = keep + lax.ppermute(away.astype(BF), axis, pairs).astype(F32)
    return current


def per_device(
    queries, cotangent, pool, enc_gain, enc_weight, k_weight, v_weight, nbr_owner, nbr_slot
):
    dp_count = lax.axis_size("dp")
    nbr_count = lax.axis_size("nbr")
    me = lax.axis_index("dp")
    held, tokens, enc_width = pool.shape
    per_row = nbr_owner.shape[0] // dp_count

    owners = nbr_owner[:, 0].reshape(dp_count, per_row)
    slots = nbr_slot[:, 0].reshape(dp_count, per_row)
    same = owners[:, :, None] == owners[:, None, :]
    earlier = jnp.tril(jnp.ones((per_row, per_row), jnp.bool_), -1)
    rank = jnp.sum((same & earlier[None]).astype(jnp.int32), axis=-1)

    ranks = jnp.arange(CAP, dtype=jnp.int32)
    blocks = jnp.arange(held, dtype=jnp.int32)
    mine = (owners == me)[:, None, :] & (rank[:, None, :] == ranks[None, :, None])
    send = jnp.any(
        mine[:, :, None, :] & (slots[:, None, None, :] == blocks[None, None, :, None]), axis=-1
    ).reshape(dp_count * CAP, held)
    enc = encode(pool.reshape(held * tokens, enc_width), enc_gain, enc_weight)
    outgoing = pick_rows(send, enc, tokens)
    arrived = lax.all_to_all(outgoing, "dp", split_axis=0, concat_axis=0, tiled=True)

    q_rows = exchange(queries, "nbr", 1, 0)
    arrived, q_rows = lax.optimization_barrier((arrived, q_rows))

    place = lax.dynamic_slice_in_dim(owners * CAP + rank, me, 1, 0)[0]
    take = place[:, None] == jnp.arange(dp_count * CAP, dtype=jnp.int32)[None, :]
    picked = pick_rows(take, arrived, tokens)
    flat_enc = lax.all_gather(picked, "nbr", axis=0, tiled=True)

    g_rows = exchange(cotangent, "nbr", 1, 0)
    seq_len, width = q_rows.shape
    lead = GROUP - 1
    blank = jnp.zeros((lead, width), BF)
    q_rows = jnp.concatenate([q_rows[lead:], blank], axis=0)
    g_rows = jnp.concatenate([g_rows[lead:], blank], axis=0)

    shape4 = (nbr_count, per_row, tokens, width)
    keys = jnp.dot(flat_enc, k_weight, preferred_element_type=F32).astype(BF)
    values = jnp.dot(flat_enc, v_weight, preferred_element_type=F32).astype(BF)
    out, dk, dv = attention(q_rows, g_rows, keys.reshape(shape4), values.reshape(shape4))

    over_first = (((0,), (0,)), ((), ()))

    def weight_grad(grads):
        return lax.dot_general(
            flat_enc, grads.reshape(-1, width), over_first, preferred_element_type=F32
        )

    grad_v = halving(weight_grad(dv), "dp", 0)
    grad_k = halving(weight_grad(dk), "dp", 1)
    out = jnp.concatenate([blank, out[: seq_len - lead]], axis=0)
    merged = exchange(out, "nbr", 0, 1)
    return (merged, grad_k, grad_v)


def solution(mesh):
    return jax.shard_map(
        per_device,
        mesh=mesh,
        in_specs=(
            P(("dp", "nbr"), None),
            P(("dp", "nbr"), None),
            P("dp", "nbr", None),
            P(),
            P(),
            P(None, "nbr"),
            P(None, "nbr"),
            P(),
            P(),
        ),
        out_specs=(P(("dp", "nbr"), None), P("dp", "nbr"), P("dp", "nbr")),
        check_vma=False,
    )
```
